32 devices in a mesh: section: 4 (over y, x), fsdp: 8 (over z, core).
Axes of the slice: x: 2, y: 2, z: 4, core: 2. Of those that a mesh axis runs over, the one named last changes fastest.
Arguments:
- inputs: bfloat16 [2, 64, 6144], P(None, None, 'fsdp'), may hold values from -6 to 6
- gains: float32 [4, 6144], P('section'), may hold values from 0.1 to 1.9
- w_qkv: bfloat16 [4, 6144, 48, 384], P('section', None, 'fsdp'), may hold values from -0.078125 to 0.078125
- layer_counts: int32 [4], P('section'), may hold values from 0 to 1, as said below
- lengths: int32 [2], replicated, may hold values from 1 to 64, as said below
Outputs:
- section_out: bfloat16 [4, 2, 64, 6144], P('section', None, None, 'fsdp')
The draws below stay inside these ranges and needn't reach their ends.
Inputs may be any that keep to these rules, and one draw needn't show every extreme that they name: `layer_counts`: some section applies 1 slots and some section applies none. `lengths`: some micro-batch has all 64 tokens valid.
All inputs are finite; a program needn't handle non-finite values.
Results may differ from the reference program's by a relative error of at most 0.02.
Values may be sent and summed in bfloat16 or wider, within the bound.
A program may use at most 128 MiB of HBM per device.

```python
import jax
import jax.numpy as jnp
from jax import lax

D = 6144
HEADS = 48
HD = 128
LMAX = 1
MB = 2
SEQ = 64
LAYERS = 4
N_SECTION = 4


def draw_layer_counts(key, part):
    counts = jax.random.randint(key, (N_SECTION,), 0, LMAX + 1).astype(jnp.int32)
    order = jax.random.permutation(jax.random.fold_in(key, 7), N_SECTION)
    places = jnp.arange(N_SECTION)
    counts = jnp.where(places == order[0], LMAX, counts)
    counts = jnp.where(places == order[1], 0, counts)
    return counts.astype(jnp.int32)


def draw_lengths(key, part):
    valid = jax.random.randint(key, (MB,), 1, SEQ + 1).astype(jnp.int32)
    chosen = jax.random.randint(jax.random.fold_in(key, 11), (), 0, MB)
    valid = jnp.where(jnp.arange(MB) == chosen, SEQ, valid)
    return valid.astype(jnp.int32)


def steps_of(rng, dims, split, least, top_value):
    level = 1.0
    for dim, shards_of in split:
        steps = jax.random.uniform(jax.random.fold_in(jax.random.fold_in(rng, 6), dim), (shards_of,), jnp.float32, least / len(split), top_value / len(split))
        level = level * jnp.repeat(jnp.exp(steps), dims[dim] // shards_of).reshape((-1,) + (1,) * (len(dims) - 1 - dim))
    return level


def scatter_about(stream_key, extent, deviation, bound, cuts=(), kind=jnp.bfloat16):
    loudness = steps_of(stream_key, extent, cuts, -0.22, 0.18) if cuts else 1.0
    result = jax.random.normal(stream_key, extent, jnp.float32) * deviation * loudness
    return jnp.minimum(jnp.maximum(result, -bound), bound).astype(kind)


def setup_inputs(seed: int = 0) -> dict:
    streams_of = jax.random.split(jax.random.key(seed), 6)
    return {
        "inputs": scatter_about(streams_of[0], (MB, SEQ, D), 1.0, 6.0, ((2, 8),)),
        "gains": jnp.clip(1.0 + 0.18 * jax.random.normal(streams_of[1], (LAYERS, D), jnp.float32), 0.1, 1.9),
        "w_qkv": scatter_about(streams_of[2], (LAYERS, D, HEADS, 3 * HD), D ** -0.5, 0.078125, ((0, 4), (2, 8))),
        "layer_counts": draw_layer_counts(jax.random.fold_in(streams_of[5], 71), 0),
        "lengths": draw_lengths(jax.random.fold_in(streams_of[5], 71), 0),
    }


def apply_layer(hidden, gain, wqkv, length):
    rows = hidden.shape[0]
    hidden_f = hidden.astype(jnp.float32)
    mean_sq = lax.optimization_barrier(jnp.mean(hidden_f * hidden_f, axis=1))
    scaled = (hidden_f * gain[None, :]).astype(jnp.bfloat16)
    projected = jnp.dot(scaled, wqkv.reshape(D, HEADS * 3 * HD), preferred_element_type=jnp.float32)
    qkv = (projected * lax.rsqrt(mean_sq + 1e-05)[:, None]).astype(jnp.bfloat16).reshape(rows, HEADS, 3 * HD)
    query = qkv[:, :, :HD].astype(jnp.float32)
    keys = qkv[:, :, HD:2 * HD].astype(jnp.float32)
    values = qkv[:, :, 2 * HD:].astype(jnp.float32)
    scores = jnp.einsum('rhd,thd->hrt', query, keys) * HD ** (-0.5)
    row_ids = lax.broadcasted_iota(jnp.int32, (rows, rows), 0)
    col_ids = lax.broadcasted_iota(jnp.int32, (rows, rows), 1)
    allowed = ((col_ids <= row_ids) & (col_ids < length))[None]
    scores = jnp.where(allowed, scores, -1e+30)
    top = lax.optimization_barrier(jnp.max(scores, axis=2, keepdims=True))
    expo = jnp.where(allowed, jnp.exp(scores - top), 0.0)
    weights = (expo / lax.optimization_barrier(jnp.sum(expo, axis=2, keepdims=True))).astype(jnp.bfloat16)
    att = jnp.einsum('hrt,thd->rhd', weights.astype(jnp.float32), values).astype(jnp.bfloat16).reshape(rows, D)
    return (hidden_f + att.astype(jnp.float32)).astype(jnp.bfloat16)

def reference(inputs, gains, w_qkv, layer_counts, lengths):
    results = []
    current = [inputs[m] for m in range(MB)]
    for section in range(N_SECTION):
        sectioned = []
        for m in range(MB):
            hidden = current[m]
            for slot in range(LMAX):
                g = section * LMAX + slot
                fresh = apply_layer(hidden, gains[g], w_qkv[g], lengths[m])
                hidden = jnp.where(slot < layer_counts[section], fresh, hidden)
            sectioned.append(hidden)
        current = sectioned
        results.append(jnp.stack(sectioned))
    return jnp.stack(results)
```

```python
import functools

import jax
import jax.numpy as jnp
from jax import lax
from jax.experimental import pallas as pl
from jax.experimental.pallas import tpu as pltpu
from jax.sharding import PartitionSpec as P

MESH = pl.DeviceIdType.MESH
F32 = jnp.float32
BF16 = jnp.bfloat16


def nearest(t, z, chips):
    near = jnp.minimum(z, chips - 1 - z)
    step = (t + 1) // 2
    both = z + jnp.where(t % 2 == 1, step, -step)
    rest = jnp.where(z <= chips - 1 - z, t, chips - 1 - t)
    return jnp.where(t <= 2 * near, both, rest)


def relay_kernel(
    chain, sections, fsdp,
    in_ref, gain_ref, w_ref, count_ref, length_ref, out_ref,
    w_vmem, gath, acc, square, res, w_sem, in_sem, recv_sem, side_send, line_send, next_send, pass_recv, pass_send,
):
    chips = fsdp // 2
    heads, span = w_ref.shape[0], w_ref.shape[2] // 3
    batches, rows, wide = in_ref.shape
    total = batches * rows
    pair = 2 if heads % 2 == 0 else 1
    sec = lax.axis_index("section")
    f = lax.axis_index("fsdp")
    z, core = f // 2, f % 2
    side = 2 * z + 1 - core
    followers = {}
    for s in range(sections):
        if s not in chain:
            before = [a for a in chain if a < s]
            followers[s] = before[-1] if before else None

    def member(group):
        found = sec == group[0]
        for other in group[1:]:
            found = found | (sec == other)
        return found

    in_chain = member(chain)

    def w_copy(g):
        part = pl.ds(pl.multiple_of(g * wide, wide), wide)
        return pltpu.make_async_copy(w_ref.at[:, part, :], w_vmem.at[:, part, :], w_sem.at[g])

    def in_copy():
        return pltpu.make_async_copy(in_ref, gath.at[f], in_sem)

    def to_side(g):
        return pltpu.make_async_remote_copy(
            src_ref=gath.at[g], dst_ref=gath.at[g], send_sem=side_send.at[g // 2], recv_sem=recv_sem.at[g],
            device_id=(sec, side), device_id_type=MESH)

    def to_line(g, way, target):
        return pltpu.make_async_remote_copy(
            src_ref=gath.at[g], dst_ref=gath.at[g], send_sem=line_send.at[way, g // 2], recv_sem=recv_sem.at[g],
            device_id=(sec, target), device_id_type=MESH)

    def to_next(b):
        return pltpu.make_async_remote_copy(
            src_ref=res, dst_ref=gath.at[f], send_sem=next_send, recv_sem=recv_sem.at[f],
            device_id=(b, f), device_id_type=MESH)

    def to_pass(s):
        return pltpu.make_async_remote_copy(
            src_ref=res, dst_ref=res, send_sem=pass_send.at[s], recv_sem=pass_recv,
            device_id=(s, f), device_id_type=MESH)

    fresh_here = member([chain[0]] + [s for s, a in followers.items() if a is None])

    @pl.when(fresh_here)
    def _():
        in_copy().start()

    @pl.when(in_chain)
    def _():
        def begin(t, carry):
            chip = nearest(t, z, chips)
            w_copy(2 * chip + core).start()
            w_copy(2 * chip + 1 - core).start()
            return carry

        lax.fori_loop(0, chips, begin, 0)

    barrier = pltpu.get_barrier_semaphore()
    pl.semaphore_signal(barrier, inc=1, device_id=(sec, side), device_id_type=MESH)
    for way, ok in ((1, z < chips - 1), (-1, z > 0)):
        @pl.when(ok)
        def _():
            pl.semaphore_signal(barrier, inc=1, device_id=(sec, f + 2 * way), device_id_type=MESH)
    for k in range(1, sections):
        pl.semaphore_signal(barrier, inc=1, device_id=((sec + k) % sections, f), device_id_type=MESH)
    ends = jnp.where(z < chips - 1, 1, 0) + jnp.where(z > 0, 1, 0)
    pl.semaphore_wait(barrier, sections + ends)

    def add_shard(g):
        w_copy(g).wait()
        part = pl.ds(pl.multiple_of(g * wide, wide), wide)
        hidden = gath[g].reshape(total, wide).astype(F32)
        square[...] += jnp.sum(hidden * hidden, axis=1, keepdims=True)
        scaled = (hidden * gain_ref[:, part]).astype(BF16)
        for p in range(heads // pair):
            weights = [w_vmem[pair * p + q, part, :] for q in range(pair)]
            weights = jnp.concatenate(weights, axis=1) if pair > 1 else weights[0]
            acc[p] += jnp.dot(scaled, weights, preferred_element_type=F32)

    @pl.when(in_chain)
    def _():
        acc[...] = jnp.zeros_like(acc)
        square[...] = jnp.zeros_like(square)

        @pl.when(sec == chain[0])
        def _():
            in_copy().wait()

        def shard(t, carry):
            chip = nearest(t, z, chips)
            g, h = 2 * chip + core, 2 * chip + 1 - core

            @pl.when((t > 0) | (sec != chain[0]))
            def _():
                to_side(g).wait_recv()

            @pl.when((chip <= z) & (z < chips - 1))
            def _():
                to_line(g, 0, f + 2).start()

            @pl.when((chip >= z) & (z > 0))
            def _():
                to_line(g, 1, f - 2).start()

            to_side(g).start()
            add_shard(g)
            to_side(h).wait_recv()
            add_shard(h)
            return carry

        lax.fori_loop(0, chips, shard, 0)

        scale = lax.rsqrt(square[...] / (wide * fsdp) + 1e-05)
        row = lax.broadcasted_iota(jnp.int32, (total, total), 0)
        col = lax.broadcasted_iota(jnp.int32, (total, total), 1)
        allowed = col < 0
        for m in range(batches):
            inside = (row >= m * rows) & (row < (m + 1) * rows) & (col >= m * rows)
            allowed = allowed | (inside & (col < m * rows + length_ref[m]))
        allowed = allowed & (col <= row)
        active = count_ref[0] > 0
        for n in range(heads):
            p, q = n // pair, n % pair
            base = 3 * span * q
            qkv = (acc[p, :, base:base + 3 * span] * scale).astype(BF16)
            scores = lax.dot_general(
                qkv[:, :span], qkv[:, span:2 * span], (((1,), (1,)), ((), ())), preferred_element_type=F32
            ) * span ** (-0.5)
            scores = jnp.where(allowed, scores, -1e30)
            expo = jnp.where(allowed, jnp.exp(scores - jnp.max(scores, axis=1, keepdims=True)), 0.0)
            weights = (expo / jnp.sum(expo, axis=1, keepdims=True)).astype(BF16)
            att = jnp.dot(weights, qkv[:, 2 * span:], preferred_element_type=F32).astype(BF16).astype(F32)
            hidden = gath[f, :, :, n * span:(n + 1) * span].reshape(total, span).astype(F32)
            fresh = jnp.where(active, hidden + att, hidden).astype(BF16)
            res[:, :, n * span:(n + 1) * span] = fresh.reshape(batches, rows, span)

        for a, b in zip(chain[:-1], chain[1:]):
            @pl.when(sec == a)
            def _():
                to_next(b).start()
        for s, a in followers.items():
            if a is not None:
                @pl.when(sec == a)
                def _():
                    to_pass(s).start()
        out_ref[...] = res[...]

        def finish(t, carry):
            g = 2 * t + core

            @pl.when((t <= z) & (z < chips - 1))
            def _():
                to_line(g, 0, f + 2).wait_send()

            @pl.when((t >= z) & (z > 0))
            def _():
                to_line(g, 1, f - 2).wait_send()

            to_side(g).wait_send()
            return carry

        lax.fori_loop(0, chips, finish, 0)
        for a, b in zip(chain[:-1], chain[1:]):
            @pl.when(sec == a)
            def _():
                to_next(b).wait_send()
        for s, a in followers.items():
            if a is not None:
                @pl.when(sec == a)
                def _():
                    to_pass(s).wait_send()

    if followers:
        @pl.when(jnp.logical_not(in_chain))
        def _():
            for s, a in followers.items():
                @pl.when(sec == s)
                def _():
                    if a is None:
                        in_copy().wait()
                        out_ref[...] = gath[f]
                    else:
                        to_pass(s).wait_recv()
                        out_ref[...] = res[...]


def relay(chain, sections, fsdp, collective, inputs, gains, w, count, lengths):
    batches, rows, wide = inputs.shape
    heads, width, cols = w.shape
    pair = 2 if heads % 2 == 0 else 1
    chips = fsdp // 2
    total = batches * rows
    dma = pltpu.SemaphoreType.DMA
    vmem = pl.BlockSpec(memory_space=pltpu.VMEM)
    smem = pl.BlockSpec(memory_space=pltpu.SMEM)
    hbm = pl.BlockSpec(memory_space=pl.ANY)
    return pl.pallas_call(
        functools.partial(relay_kernel, chain, sections, fsdp),
        out_shape=jax.ShapeDtypeStruct((batches, rows, wide), BF16),
        in_specs=[hbm, vmem, hbm, smem, smem],
        out_specs=vmem,
        scratch_shapes=[
            pltpu.VMEM((heads, width, cols), BF16),
            pltpu.VMEM((fsdp, batches, rows, wide), BF16),
            pltpu.VMEM((heads // pair, total, pair * cols), F32),
            pltpu.VMEM((total, 1), F32),
            pltpu.VMEM((batches, rows, wide), BF16),
            dma((fsdp,)),
            dma,
            dma((fsdp,)),
            dma((chips,)),
            dma((2, chips)),
            dma,
            dma,
            dma((sections,)),
        ],
        compiler_params=pltpu.CompilerParams(
            collective_id=collective, has_side_effects=True, vmem_limit_bytes=48 * 2**20
        ),
        cost_estimate=pl.CostEstimate(
            flops=2 * total * width * heads * cols, bytes_accessed=2 * heads * width * cols, transcendentals=0
        ),
    )(inputs, gains, w, count, lengths)


def solution(mesh):
    sections, fsdp = mesh.shape["section"], mesh.shape["fsdp"]

    def per_device(inputs, gains, w_qkv, layer_counts, lengths):
        w = jnp.transpose(w_qkv[0], (1, 0, 2))
        out = relay(tuple(range(sections)), sections, fsdp, 0, inputs, gains, w, layer_counts, lengths)
        return out[None]

    in_specs = (
        P(None, None, "fsdp"),
        P("section", None),
        P("section", None, "fsdp", None),
        P("section"),
        P(),
    )
    return jax.shard_map(
        per_device, mesh=mesh, in_specs=in_specs, out_specs=P("section", None, None, "fsdp"), check_vma=False
    )
```

```python
import functools

import jax
import jax.numpy as jnp
from jax import lax
from jax.experimental import pallas as pl
from jax.experimental.pallas import tpu as pltpu
from jax.sharding import PartitionSpec as P

MESH = pl.DeviceIdType.MESH
F32 = jnp.float32
BF16 = jnp.bfloat16


def nearest(t, z, chips):
    near = jnp.minimum(z, chips - 1 - z)
    step = (t + 1) // 2
    both = z + jnp.where(t % 2 == 1, step, -step)
    rest = jnp.where(z <= chips - 1 - z, t, chips - 1 - t)
    return jnp.where(t <= 2 * near, both, rest)


def relay_kernel(
    chain, sections, fsdp,
    in_ref, gain_hbm, w_ref, count_ref, length_ref, out_ref, gain_ref, gain_sem,
    w_vmem, gath, acc, square, res, w_sem, in_sem, recv_sem, side_send, line_send, next_send, pass_recv, pass_send,
):
    chips = fsdp // 2
    heads, span = w_ref.shape[0], w_ref.shape[2] // 3
    batches, rows, wide = in_ref.shape
    total = batches * rows
    pair = 2 if heads % 2 == 0 else 1
    sec = lax.axis_index("section")
    f = lax.axis_index("fsdp")
    z, core = f // 2, f % 2
    side = 2 * z + 1 - core
    followers = {}
    for s in range(sections):
        if s not in chain:
            before = [a for a in chain if a < s]
            followers[s] = before[-1] if before else None

    def member(group):
        found = sec == group[0]
        for other in group[1:]:
            found = found | (sec == other)
        return found

    in_chain = member(chain)

    def w_copy(g):
        part = pl.ds(pl.multiple_of(g * wide, wide), wide)
        return pltpu.make_async_copy(w_ref.at[:, part, :], w_vmem.at[:, part, :], w_sem.at[g])

    def gain_copy():
        return pltpu.make_async_copy(gain_hbm, gain_ref, gain_sem)

    def in_copy():
        return pltpu.make_async_copy(in_ref, gath.at[f], in_sem)

    def to_side(g):
        return pltpu.make_async_remote_copy(
            src_ref=gath.at[g], dst_ref=gath.at[g], send_sem=side_send.at[g // 2], recv_sem=recv_sem.at[g],
            device_id=(sec, side), device_id_type=MESH)

    def to_line(g, way, target):
        return pltpu.make_async_remote_copy(
            src_ref=gath.at[g], dst_ref=gath.at[g], send_sem=line_send.at[way, g // 2], recv_sem=recv_sem.at[g],
            device_id=(sec, target), device_id_type=MESH)

    def to_next(b):
        return pltpu.make_async_remote_copy(
            src_ref=res, dst_ref=gath.at[f], send_sem=next_send, recv_sem=recv_sem.at[f],
            device_id=(b, f), device_id_type=MESH)

    def to_pass(s):
        return pltpu.make_async_remote_copy(
            src_ref=res, dst_ref=res, send_sem=pass_send.at[s], recv_sem=pass_recv,
            device_id=(s, f), device_id_type=MESH)

    fresh_here = member([chain[0]] + [s for s, a in followers.items() if a is None])

    @pl.when(fresh_here)
    def _():
        in_copy().start()

    @pl.when(in_chain)
    def _():
        def begin(t, carry):
            chip = nearest(t, z, chips)
            w_copy(2 * chip + core).start()
            w_copy(2 * chip + 1 - core).start()
            return carry

        gain_copy().start()
        lax.fori_loop(0, chips, begin, 0)

    barrier = pltpu.get_barrier_semaphore()
    pl.semaphore_signal(barrier, inc=1, device_id=(sec, side), device_id_type=MESH)
    for way, ok in ((1, z < chips - 1), (-1, z > 0)):
        @pl.when(ok)
        def _():
            pl.semaphore_signal(barrier, inc=1, device_id=(sec, f + 2 * way), device_id_type=MESH)
    for k in range(1, sections):
        pl.semaphore_signal(barrier, inc=1, device_id=((sec + k) % sections, f), device_id_type=MESH)
    ends = jnp.where(z < chips - 1, 1, 0) + jnp.where(z > 0, 1, 0)
    pl.semaphore_wait(barrier, sections + ends)

    def add_shard(g):
        w_copy(g).wait()
        part = pl.ds(pl.multiple_of(g * wide, wide), wide)
        hidden = gath[g].reshape(total, wide).astype(F32)
        square[...] += jnp.sum(hidden * hidden, axis=1, keepdims=True)
        scaled = (hidden * gain_ref[:, part]).astype(BF16)
        for p in range(heads // pair):
            weights = [w_vmem[pair * p + q, part, :] for q in range(pair)]
            weights = jnp.concatenate(weights, axis=1) if pair > 1 else weights[0]
            acc[p] += jnp.dot(scaled, weights, preferred_element_type=F32)

    @pl.when(in_chain)
    def _():
        acc[...] = jnp.zeros_like(acc)
        square[...] = jnp.zeros_like(square)
        gain_copy().wait()

        @pl.when(sec == chain[0])
        def _():
            in_copy().wait()

        def shard(t, carry):
            chip = nearest(t, z, chips)
            g, h = 2 * chip + core, 2 * chip + 1 - core

            @pl.when((t > 0) | (sec != chain[0]))
            def _():
                to_side(g).wait_recv()

            @pl.when((chip <= z) & (z < chips - 1))
            def _():
                to_line(g, 0, f + 2).start()

            @pl.when((chip >= z) & (z > 0))
            def _():
                to_line(g, 1, f - 2).start()

            to_side(g).start()
            add_shard(g)
            to_side(h).wait_recv()
            add_shard(h)
            return carry

        lax.fori_loop(0, chips, shard, 0)

        scale = lax.rsqrt(square[...] / (wide * fsdp) + 1e-05)
        row = lax.broadcasted_iota(jnp.int32, (total, total), 0)
        col = lax.broadcasted_iota(jnp.int32, (total, total), 1)
        allowed = col < 0
        for m in range(batches):
            inside = (row >= m * rows) & (row < (m + 1) * rows) & (col >= m * rows)
            allowed = allowed | (inside & (col < m * rows + length_ref[m]))
        allowed = allowed & (col <= row)
        active = count_ref[0] > 0
        for n in range(heads):
            p, q = n // pair, n % pair
            base = 3 * span * q
            qkv = (acc[p, :, base:base + 3 * span] * scale).astype(BF16)
            scores = lax.dot_general(
                qkv[:, :span], qkv[:, span:2 * span], (((1,), (1,)), ((), ())), preferred_element_type=F32
            ) * span ** (-0.5)
            scores = jnp.where(allowed, scores, -1e30)
            expo = jnp.where(allowed, jnp.exp(scores - jnp.max(scores, axis=1, keepdims=True)), 0.0)
            weights = (expo / jnp.sum(expo, axis=1, keepdims=True)).astype(BF16)
            att = jnp.dot(weights, qkv[:, 2 * span:], preferred_element_type=F32).astype(BF16).astype(F32)
            hidden = gath[f, :, :, n * span:(n + 1) * span].reshape(total, span).astype(F32)
            fresh = jnp.where(active, hidden + att, hidden).astype(BF16)
            res[:, :, n * span:(n + 1) * span] = fresh.reshape(batches, rows, span)

        for a, b in zip(chain[:-1], chain[1:]):
            @pl.when(sec == a)
            def _():
                to_next(b).start()
        for s, a in followers.items():
            if a is not None:
                @pl.when(sec == a)
                def _():
                    to_pass(s).start()
        out_ref[...] = res[...]

        def finish(t, carry):
            g = 2 * t + core

            @pl.when((t <= z) & (z < chips - 1))
            def _():
                to_line(g, 0, f + 2).wait_send()

            @pl.when((t >= z) & (z > 0))
            def _():
                to_line(g, 1, f - 2).wait_send()

            to_side(g).wait_send()
            return carry

        lax.fori_loop(0, chips, finish, 0)
        for a, b in zip(chain[:-1], chain[1:]):
            @pl.when(sec == a)
            def _():
                to_next(b).wait_send()
        for s, a in followers.items():
            if a is not None:
                @pl.when(sec == a)
                def _():
                    to_pass(s).wait_send()

    if followers:
        @pl.when(jnp.logical_not(in_chain))
        def _():
            for s, a in followers.items():
                @pl.when(sec == s)
                def _():
                    if a is None:
                        in_copy().wait()
                        out_ref[...] = gath[f]
                    else:
                        to_pass(s).wait_recv()
                        out_ref[...] = res[...]


def relay(chain, sections, fsdp, collective, inputs, gains, w, count, lengths):
    batches, rows, wide = inputs.shape
    heads, width, cols = w.shape
    pair = 2 if heads % 2 == 0 else 1
    chips = fsdp // 2
    total = batches * rows
    dma = pltpu.SemaphoreType.DMA
    scratch_gain = pltpu.VMEM(gains.shape, F32)
    vmem = pl.BlockSpec(memory_space=pltpu.VMEM)
    smem = pl.BlockSpec(memory_space=pltpu.SMEM)
    hbm = pl.BlockSpec(memory_space=pltpu.HBM)
    return pl.pallas_call(
        functools.partial(relay_kernel, chain, sections, fsdp),
        out_shape=jax.ShapeDtypeStruct((batches, rows, wide), BF16),
        in_specs=[hbm, hbm, hbm, smem, smem],
        out_specs=vmem,
        scratch_shapes=[
            scratch_gain,
            dma,
            pltpu.VMEM((heads, width, cols), BF16),
            pltpu.VMEM((fsdp, batches, rows, wide), BF16),
            pltpu.VMEM((heads // pair, total, pair * cols), F32),
            pltpu.VMEM((total, 1), F32),
            pltpu.VMEM((batches, rows, wide), BF16),
            dma((fsdp,)),
            dma,
            dma((fsdp,)),
            dma((chips,)),
            dma((2, chips)),
            dma,
            dma,
            dma((sections,)),
        ],
        compiler_params=pltpu.CompilerParams(
            collective_id=collective, has_side_effects=True, vmem_limit_bytes=48 * 2**20
        ),
        cost_estimate=pl.CostEstimate(
            flops=2 * total * width * heads * cols, bytes_accessed=2 * heads * width * cols, transcendentals=0
        ),
    )(inputs, gains, w, count, lengths)


def pattern_kernel(sections, count_ref, found_ref, slots, send_sem, recv_sem):
    sec = lax.axis_index("section")
    f = lax.axis_index("fsdp")
    slots[sec] = jnp.full(slots.shape[1:], jnp.where(count_ref[0] > 0, 1, 0), jnp.int32)
    barrier = pltpu.get_barrier_semaphore()
    for k in range(1, sections):
        pl.semaphore_signal(barrier, inc=1, device_id=((sec + k) % sections, f), device_id_type=MESH)
    pl.semaphore_wait(barrier, sections - 1)

    def tell(k):
        return pltpu.make_async_remote_copy(
            src_ref=slots.at[sec], dst_ref=slots.at[sec], send_sem=send_sem.at[k], recv_sem=recv_sem.at[k],
            device_id=((sec + k) % sections, f), device_id_type=MESH)

    for k in range(1, sections):
        tell(k).start()
    for k in range(1, sections):
        tell(k).wait()
    found = jnp.zeros(slots.shape[1:], jnp.int32)
    for s in range(sections):
        found = found + slots[s] * 2**s
    found_ref[...] = found


def pattern(sections, count):
    dma = pltpu.SemaphoreType.DMA
    found = pl.pallas_call(
        functools.partial(pattern_kernel, sections),
        out_shape=jax.ShapeDtypeStruct((8, 128), jnp.int32),
        in_specs=[pl.BlockSpec(memory_space=pltpu.SMEM)],
        out_specs=pl.BlockSpec(memory_space=pltpu.VMEM),
        scratch_shapes=[pltpu.VMEM((sections, 8, 128), jnp.int32), dma((sections,)), dma((sections,))],
        compiler_params=pltpu.CompilerParams(collective_id=0, has_side_effects=True),
    )(count)
    return found[0, 0]


def solution(mesh):
    sections, fsdp = mesh.shape["section"], mesh.shape["fsdp"]

    def per_device(inputs, gains, w_qkv, layer_counts, lengths):
        w = jnp.transpose(w_qkv[0], (1, 0, 2))
        operands = (inputs, gains, w, layer_counts, lengths)
        if sections > 4:
            return relay(tuple(range(sections)), sections, fsdp, 0, *operands)[None]
        branches = []
        for bits in range(1, 2**sections - 1):
            chain = tuple(s for s in range(sections) if bits >> s & 1)
            branches.append(functools.partial(relay, chain, sections, fsdp, bits))
        out = lax.switch(pattern(sections, layer_counts) - 1, branches, *operands)
        return out[None]

    in_specs = (
        P(None, None, "fsdp"),
        P("section", None),
        P("section", None, "fsdp", None),
        P("section"),
        P(),
    )
    return jax.shard_map(
        per_device, mesh=mesh, in_specs=in_specs, out_specs=P("section", None, None, "fsdp"), check_vma=False
    )
```

```python
import functools

import jax
import jax.numpy as jnp
from jax import lax
from jax.experimental import pallas as pl
from jax.experimental.pallas import tpu as pltpu
from jax.sharding import PartitionSpec as P

MESH = pl.DeviceIdType.MESH
F32 = jnp.float32
BF16 = jnp.bfloat16


def nearest(t, z, chips):
    near = jnp.minimum(z, chips - 1 - z)
    step = (t + 1) // 2
    both = z + jnp.where(t % 2 == 1, step, -step)
    rest = jnp.where(z <= chips - 1 - z, t, chips - 1 - t)
    return jnp.where(t <= 2 * near, both, rest)


def relay_kernel(
    chain, sections, fsdp,
    in_ref, gain_hbm, w_ref, count_ref, length_ref, out_ref,
    gain_ref, w_vmem, gath, relayed, acc, square, res,
    gain_sem, w_sem, in_sem, recv_sem, side_recv, side_send, line_send,
    relay_recv, relay_send, cross_send, next_send, pass_recv, pass_send,
):
    chips = fsdp // 2
    heads, span = w_ref.shape[0], w_ref.shape[2] // 3
    batches, rows, wide = in_ref.shape
    total = batches * rows
    pair = 2 if heads % 2 == 0 else 1
    sec = lax.axis_index("section")
    f = lax.axis_index("fsdp")
    z, core = f // 2, f % 2
    side = 2 * z + 1 - core
    helper = chain[0] ^ 1
    followers = {}
    for s in range(sections):
        if s not in chain:
            before = [a for a in chain if a < s]
            followers[s] = before[-1] if before else None

    def member(group):
        found = sec == group[0]
        for other in group[1:]:
            found = found | (sec == other)
        return found

    in_chain = member(chain)

    def remote(src, dst, send, recv, target):
        return pltpu.make_async_remote_copy(
            src_ref=src, dst_ref=dst, send_sem=send, recv_sem=recv, device_id=target, device_id_type=MESH)

    def w_copy(chip):
        part = pl.ds(pl.multiple_of(chip * 2 * wide, 2 * wide), 2 * wide)
        return pltpu.make_async_copy(w_ref.at[:, part, :], w_vmem.at[:, part, :], w_sem.at[chip])

    def gain_copy():
        return pltpu.make_async_copy(gain_hbm, gain_ref, gain_sem)

    def in_copy():
        return pltpu.make_async_copy(in_ref, gath.at[f], in_sem)

    def to_side(g):
        return remote(gath.at[g], gath.at[g], side_send.at[g // 2], side_recv.at[g], (sec, side))

    def to_line(chip):
        return remote(gath.at[f, 1], gath.at[f, 1], line_send.at[chip], recv_sem.at[1, f], (sec, 2 * chip + core))

    def arrival(m, g):
        return remote(gath.at[g, m], gath.at[g, m], line_send.at[0], recv_sem.at[m, g], (sec, side))

    def relay_line(turn, src, chip):
        return remote(
            src, relayed.at[turn, z], relay_send.at[turn, chip], relay_recv.at[turn, z], (sec, 2 * chip + core))

    def relay_arrival(turn, chip):
        return remote(
            relayed.at[turn, chip], relayed.at[turn, chip], relay_send.at[turn, chip], relay_recv.at[turn, chip],
            (sec, side))

    def cross(turn, src, chip, b):
        g = 2 * chip + core
        return remote(src, gath.at[g, 0], cross_send.at[turn, chip], recv_sem.at[0, g], (b, f))

    def to_next(b):
        return remote(res.at[1], gath.at[f, 1], next_send, recv_sem.at[1, f], (b, f))

    def to_pass(s):
        return remote(res, res, pass_send.at[s], pass_recv, (s, f))

    def others(body):
        def step(t, carry):
            body(nearest(t, z, chips))
            return carry

        lax.fori_loop(1, chips, step, 0)

    def relay_cross(turn, b):
        def body(chip):
            relay_arrival(turn, chip).wait_recv()
            cross(turn, relayed.at[turn, chip], chip, b).start()

        others(body)

    def relay_finish(turn, src, b):
        def body(chip):
            relay_line(turn, src, chip).wait_send()
            cross(turn, relayed.at[turn, chip], chip, b).wait_send()

        others(body)

    fresh_here = member([chain[0]] + [s for s, a in followers.items() if a is None])

    @pl.when(fresh_here)
    def _():
        in_copy().start()

    @pl.when(in_chain)
    def _():
        def begin(t, carry):
            w_copy(nearest(t, z, chips)).start()
            return carry

        gain_copy().start()
        lax.fori_loop(0, chips, begin, 0)

    barrier = pltpu.get_barrier_semaphore()
    pl.semaphore_signal(barrier, inc=1, device_id=(sec, side), device_id_type=MESH)
    others(lambda chip: pl.semaphore_signal(
        barrier, inc=1, device_id=(sec, 2 * chip + core), device_id_type=MESH))
    for k in range(1, sections):
        pl.semaphore_signal(barrier, inc=1, device_id=((sec + k) % sections, f), device_id_type=MESH)
    pl.semaphore_wait(barrier, sections + chips - 1)

    @pl.when(sec == helper)
    def _():
        others(lambda chip: relay_line(0, in_ref.at[0], chip).start())
        relay_cross(0, chain[0])

    @pl.when(in_chain)
    def _():
        acc[...] = jnp.zeros_like(acc)
        square[...] = jnp.zeros_like(square)
        gain_copy().wait()

        @pl.when(sec == chain[0])
        def _():
            in_copy().wait()

        if len(chain) > 1:
            @pl.when(sec != chain[0])
            def _():
                arrival(1, f).wait_recv()

        others(lambda chip: to_line(chip).start())

        def step(t, carry):
            chip = nearest(t, z, chips)
            g, h = 2 * chip + core, 2 * chip + 1 - core

            @pl.when((t > 0) | (sec != chain[0]))
            def _():
                arrival(0, g).wait_recv()

            @pl.when(t > 0)
            def _():
                arrival(1, g).wait_recv()

            to_side(g).start()
            w_copy(chip).wait()
            to_side(h).wait_recv()
            part = pl.ds(pl.multiple_of(chip * 2 * wide, 2 * wide), 2 * wide)
            both = [gath[2 * chip + q].reshape(total, wide).astype(F32) for q in range(2)]
            hidden = jnp.concatenate(both, axis=1)
            square[...] += jnp.sum(hidden * hidden, axis=1, keepdims=True)
            scaled = (hidden * gain_ref[:, part]).astype(BF16)
            for p in range(heads // pair):
                weights = [w_vmem[pair * p + q, part, :] for q in range(pair)]
                weights = jnp.concatenate(weights, axis=1) if pair > 1 else weights[0]
                acc[p] += jnp.dot(scaled, weights, preferred_element_type=F32)
            return carry

        lax.fori_loop(0, chips, step, 0)

        scale = lax.rsqrt(square[...] / (wide * fsdp) + 1e-05)
        row = lax.broadcasted_iota(jnp.int32, (total, total), 0)
        col = lax.broadcasted_iota(jnp.int32, (total, total), 1)
        allowed = col < 0
        for m in range(batches):
            inside = (row >= m * rows) & (row < (m + 1) * rows) & (col >= m * rows)
            allowed = allowed | (inside & (col < m * rows + length_ref[m]))
        allowed = allowed & (col <= row)
        active = count_ref[0] > 0
        qkvs, exps, atts = [], [], []
        for n in range(heads):
            base = 3 * span * (n % pair)
            qkvs.append((acc[n // pair, :, base:base + 3 * span] * scale).astype(BF16))
        scores = [
            lax.dot_general(
                qkv[:, :span], qkv[:, span:2 * span], (((1,), (1,)), ((), ())), preferred_element_type=F32
            ) for qkv in qkvs
        ]
        for score in scores:
            score = jnp.where(allowed, score * span ** (-0.5), -1e30)
            exps.append(jnp.where(allowed, jnp.exp(score - jnp.max(score, axis=1, keepdims=True)), 0.0))
        for expo, qkv in zip(exps, qkvs):
            weights = (expo * (1.0 / jnp.sum(expo, axis=1, keepdims=True))).astype(BF16)
            atts.append(jnp.dot(weights, qkv[:, 2 * span:], preferred_element_type=F32))
        for n in range(heads):
            att = atts[n].astype(BF16).astype(F32)
            hidden = gath[f, :, :, n * span:(n + 1) * span].reshape(total, span).astype(F32)
            fresh = jnp.where(active, hidden + att, hidden).astype(BF16)
            res[:, :, n * span:(n + 1) * span] = fresh.reshape(batches, rows, span)

        links = list(zip(chain[:-1], chain[1:]))
        for a, b in links:
            @pl.when(sec == a)
            def _():
                to_next(b).start()
                cross(1, res.at[0], z, b).start()
        if links:
            @pl.when(sec != chain[-1])
            def _():
                others(lambda chip: relay_line(1, res.at[0], chip).start())
        for s, a in followers.items():
            if a is not None:
                @pl.when(sec == a)
                def _():
                    to_pass(s).start()
        out_ref[...] = res[...]
        for a, b in links:
            @pl.when(sec == a)
            def _():
                relay_cross(1, b)

        others(lambda chip: to_line(chip).wait_send())

        def finish(t, carry):
            to_side(2 * t + core).wait_send()
            return carry

        lax.fori_loop(0, chips, finish, 0)
        for a, b in links:
            @pl.when(sec == a)
            def _():
                to_next(b).wait_send()
                cross(1, res.at[0], z, b).wait_send()
                relay_finish(1, res.at[0], b)
        for s, a in followers.items():
            if a is not None:
                @pl.when(sec == a)
                def _():
                    to_pass(s).wait_send()

    for s, a in followers.items():
        @pl.when(sec == s)
        def _():
            if a is None:
                in_copy().wait()
                out_ref[...] = gath[f]
            else:
                to_pass(s).wait_recv()
                out_ref[...] = res[...]

    @pl.when(sec == helper)
    def _():
        relay_finish(0, in_ref.at[0], chain[0])


def relay(chain, sections, fsdp, collective, inputs, gains, w, count, lengths):
    batches, rows, wide = inputs.shape
    heads, width, cols = w.shape
    pair = 2 if heads % 2 == 0 else 1
    chips = fsdp // 2
    total = batches * rows
    dma = pltpu.SemaphoreType.DMA
    vmem = pl.BlockSpec(memory_space=pltpu.VMEM)
    smem = pl.BlockSpec(memory_space=pltpu.SMEM)
    hbm = pl.BlockSpec(memory_space=pltpu.HBM)
    return pl.pallas_call(
        functools.partial(relay_kernel, chain, sections, fsdp),
        out_shape=jax.ShapeDtypeStruct((batches, rows, wide), BF16),
        in_specs=[hbm, hbm, hbm, smem, smem],
        out_specs=vmem,
        scratch_shapes=[
            pltpu.VMEM(gains.shape, F32),
            pltpu.VMEM((heads, width, cols), BF16),
            pltpu.VMEM((fsdp, batches, rows, wide), BF16),
            pltpu.VMEM((2, chips, rows, wide), BF16),
            pltpu.VMEM((heads // pair, total, pair * cols), F32),
            pltpu.VMEM((total, 1), F32),
            pltpu.VMEM((batches, rows, wide), BF16),
            dma,
            dma((chips,)),
            dma,
            dma((batches, fsdp)),
            dma((fsdp,)),
            dma((chips,)),
            dma((chips,)),
            dma((2, chips)),
            dma((2, chips)),
            dma((2, chips)),
            dma,
            dma,
            dma((sections,)),
        ],
        compiler_params=pltpu.CompilerParams(
            collective_id=collective, has_side_effects=True, vmem_limit_bytes=48 * 2**20
        ),
        cost_estimate=pl.CostEstimate(
            flops=2 * total * width * heads * cols, bytes_accessed=2 * heads * width * cols, transcendentals=0
        ),
    )(inputs, gains, w, count, lengths)


def pattern_kernel(sections, count_ref, found_ref, slots, counts, copy_sem, send_sem, recv_sem):
    sec = lax.axis_index("section")
    f = lax.axis_index("fsdp")
    slots[sec] = jnp.full(slots.shape[1:], jnp.where(count_ref[0] > 0, 1, 0), jnp.int32)
    barrier = pltpu.get_barrier_semaphore()
    for k in range(1, sections):
        pl.semaphore_signal(barrier, inc=1, device_id=((sec + k) % sections, f), device_id_type=MESH)
    pl.semaphore_wait(barrier, sections - 1)

    def tell(k):
        return pltpu.make_async_remote_copy(
            src_ref=slots.at[sec], dst_ref=slots.at[sec], send_sem=send_sem.at[k], recv_sem=recv_sem.at[k],
            device_id=((sec + k) % sections, f), device_id_type=MESH)

    for k in range(1, sections):
        tell(k).start()
    for k in range(1, sections):
        tell(k).wait()
    copy = pltpu.make_async_copy(slots, counts, copy_sem)
    copy.start()
    copy.wait()
    found = -1
    for s in range(sections):
        found = found + counts[s, 0, 0] * 2**s
    found_ref[0] = found


def pattern(sections, count):
    dma = pltpu.SemaphoreType.DMA
    found = pl.pallas_call(
        functools.partial(pattern_kernel, sections),
        out_shape=jax.ShapeDtypeStruct((1,), jnp.int32),
        in_specs=[pl.BlockSpec(memory_space=pltpu.SMEM)],
        out_specs=pl.BlockSpec(memory_space=pltpu.SMEM),
        scratch_shapes=[
            pltpu.VMEM((sections, 8, 128), jnp.int32),
            pltpu.SMEM((sections, 8, 128), jnp.int32),
            dma,
            dma((sections,)),
            dma((sections,)),
        ],
        compiler_params=pltpu.CompilerParams(collective_id=0, has_side_effects=True),
    )(count)
    return found[0]


def solution(mesh):
    sections, fsdp = mesh.shape["section"], mesh.shape["fsdp"]

    def per_device(inputs, gains, w_qkv, layer_counts, lengths):
        w = jnp.transpose(w_qkv[0], (1, 0, 2))
        operands = (inputs, gains, w, layer_counts, lengths)
        if sections > 4:
            return relay(tuple(range(sections)), sections, fsdp, 0, *operands)[None]
        branches = []
        for bits in range(1, 2**sections - 1):
            chain = tuple(s for s in range(sections) if bits >> s & 1)
            branches.append(functools.partial(relay, chain, sections, fsdp, bits))
        out = lax.switch(pattern(sections, layer_counts), branches, *operands)
        return out[None]

    in_specs = (
        P(None, None, "fsdp"),
        P("section", None),
        P("section", None, "fsdp", None),
        P("section"),
        P(),
    )
    return jax.shard_map(
        per_device, mesh=mesh, in_specs=in_specs, out_specs=P("section", None, None, "fsdp"), check_vma=False
    )
```

```python
import functools

import jax
import jax.numpy as jnp
from jax import lax
from jax.experimental import pallas as pl
from jax.experimental.pallas import tpu as pltpu
from jax.sharding import PartitionSpec as P

MESH = pl.DeviceIdType.MESH
F32 = jnp.float32
BF16 = jnp.bfloat16


def nearest(t, z, chips):
    near = jnp.minimum(z, chips - 1 - z)
    step = (t + 1) // 2
    both = z + jnp.where(t % 2 == 1, step, -step)
    rest = jnp.where(z <= chips - 1 - z, t, chips - 1 - t)
    return jnp.where(t <= 2 * near, both, rest)


def relay_kernel(
    chain, sections, fsdp,
    in_ref, gain_hbm, w_ref, count_ref, length_ref, out_ref,
    gain_ref, w_vmem, gath, relayed, acc, square, res,
    gain_sem, w_sem, in_sem, recv_sem, side_recv, side_send, line_send,
    relay_recv, relay_send, cross_send, next_send, pass_recv, pass_send,
):
    chips = fsdp // 2
    heads, span = w_ref.shape[0], w_ref.shape[2] // 3
    blocks, lanes = w_vmem.shape[0], w_vmem.shape[3]
    batches, rows, wide = in_ref.shape
    total = batches * rows
    pair = 2 if heads % 2 == 0 else 1
    sec = lax.axis_index("section")
    f = lax.axis_index("fsdp")
    z, core = f // 2, f % 2
    side = 2 * z + 1 - core
    helper = chain[0] ^ 1
    followers = {}
    for s in range(sections):
        if s not in chain:
            before = [a for a in chain if a < s]
            followers[s] = before[-1] if before else None

    def member(group):
        found = sec == group[0]
        for other in group[1:]:
            found = found | (sec == other)
        return found

    in_chain = member(chain)

    def remote(src, dst, send, recv, target):
        return pltpu.make_async_remote_copy(
            src_ref=src, dst_ref=dst, send_sem=send, recv_sem=recv, device_id=target, device_id_type=MESH)

    def w_copy(chip, c):
        part = pl.ds(pl.multiple_of(chip * 2 * wide, 2 * wide), 2 * wide)
        return pltpu.make_async_copy(
            w_ref.at[:, part, c * lanes:(c + 1) * lanes], w_vmem.at[c, :, part, :], w_sem.at[chip, c])

    def gain_copy():
        return pltpu.make_async_copy(gain_hbm, gain_ref, gain_sem)

    def in_copy():
        return pltpu.make_async_copy(in_ref, gath.at[f], in_sem)

    def to_side(g):
        return remote(gath.at[g], gath.at[g], side_send.at[g // 2], side_recv.at[g], (sec, side))

    def to_line(chip):
        return remote(gath.at[f, 1], gath.at[f, 1], line_send.at[chip], recv_sem.at[1, f], (sec, 2 * chip + core))

    def arrival(m, g):
        return remote(gath.at[g, m], gath.at[g, m], line_send.at[0], recv_sem.at[m, g], (sec, side))

    def relay_line(turn, src, chip):
        return remote(
            src, relayed.at[turn, z], relay_send.at[turn, chip], relay_recv.at[turn, z], (sec, 2 * chip + core))

    def relay_arrival(turn, chip):
        return remote(
            relayed.at[turn, chip], relayed.at[turn, chip], relay_send.at[turn, chip], relay_recv.at[turn, chip],
            (sec, side))

    def cross(turn, src, chip, b):
        g = 2 * chip + core
        return remote(src, gath.at[g, 0], cross_send.at[turn, chip], recv_sem.at[0, g], (b, f))

    def to_next(b):
        return remote(res.at[1], gath.at[f, 1], next_send, recv_sem.at[1, f], (b, f))

    def to_pass(s):
        return remote(res, res, pass_send.at[s], pass_recv, (s, f))

    def others(body):
        def step(t, carry):
            body(nearest(t, z, chips))
            return carry

        lax.fori_loop(1, chips, step, 0)

    def relay_cross(turn, b):
        def body(chip):
            relay_arrival(turn, chip).wait_recv()
            cross(turn, relayed.at[turn, chip], chip, b).start()

        others(body)

    def relay_finish(turn, src, b):
        def body(chip):
            relay_line(turn, src, chip).wait_send()
            cross(turn, relayed.at[turn, chip], chip, b).wait_send()

        others(body)

    fresh_here = member([chain[0]] + [s for s, a in followers.items() if a is None])

    @pl.when(fresh_here)
    def _():
        in_copy().start()

    @pl.when(in_chain)
    def _():
        def begin(t, carry):
            for c in range(blocks):
                w_copy(nearest(t, z, chips), c).start()
            return carry

        gain_copy().start()
        lax.fori_loop(0, chips, begin, 0)

    barrier = pltpu.get_barrier_semaphore()
    pl.semaphore_signal(barrier, inc=1, device_id=(sec, side), device_id_type=MESH)
    others(lambda chip: pl.semaphore_signal(
        barrier, inc=1, device_id=(sec, 2 * chip + core), device_id_type=MESH))
    for k in range(1, sections):
        pl.semaphore_signal(barrier, inc=1, device_id=((sec + k) % sections, f), device_id_type=MESH)
    pl.semaphore_wait(barrier, sections + chips - 1)

    @pl.when(sec == helper)
    def _():
        others(lambda chip: relay_line(0, in_ref.at[0], chip).start())
        relay_cross(0, chain[0])

    @pl.when(in_chain)
    def _():
        acc[...] = jnp.zeros_like(acc)
        square[...] = jnp.zeros_like(square)
        gain_copy().wait()

        @pl.when(sec == chain[0])
        def _():
            in_copy().wait()

        if len(chain) > 1:
            @pl.when(sec != chain[0])
            def _():
                arrival(1, f).wait_recv()

        others(lambda chip: to_line(chip).start())

        def step(t, carry):
            chip = nearest(t, z, chips)
            g, h = 2 * chip + core, 2 * chip + 1 - core

            @pl.when((t > 0) | (sec != chain[0]))
            def _():
                arrival(0, g).wait_recv()

            @pl.when(t > 0)
            def _():
                arrival(1, g).wait_recv()

            to_side(g).start()
            for c in range(blocks):
                w_copy(chip, c).wait()
            to_side(h).wait_recv()
            part = pl.ds(pl.multiple_of(chip * 2 * wide, 2 * wide), 2 * wide)
            both = [gath[2 * chip + q].reshape(total, wide).astype(F32) for q in range(2)]
            hidden = jnp.concatenate(both, axis=1)
            square[...] += jnp.sum(hidden * hidden, axis=1, keepdims=True)
            scaled = (hidden * gain_ref[:, part]).astype(BF16)
            for p in range(heads // pair):
                weights = [w_vmem[c, pair * p + q, part, :] for q in range(pair) for c in range(blocks)]
                weights = jnp.concatenate(weights, axis=1)
                acc[p] += jnp.dot(scaled, weights, preferred_element_type=F32)
            return carry

        lax.fori_loop(0, chips, step, 0)

        scale = lax.rsqrt(square[...] / (wide * fsdp) + 1e-05)
        row = lax.broadcasted_iota(jnp.int32, (total, total), 0)
        col = lax.broadcasted_iota(jnp.int32, (total, total), 1)
        allowed = col < 0
        for m in range(batches):
            inside = (row >= m * rows) & (row < (m + 1) * rows) & (col >= m * rows)
            allowed = allowed | (inside & (col < m * rows + length_ref[m]))
        allowed = allowed & (col <= row)
        active = count_ref[0] > 0
        qkvs, exps, atts = [], [], []
        for n in range(heads):
            base = 3 * span * (n % pair)
            qkvs.append((acc[n // pair, :, base:base + 3 * span] * scale).astype(BF16))
        scores = [
            lax.dot_general(
                qkv[:, :span], qkv[:, span:2 * span], (((1,), (1,)), ((), ())), preferred_element_type=F32
            ) for qkv in qkvs
        ]
        for score in scores:
            score = jnp.where(allowed, score * span ** (-0.5), -1e30)
            exps.append(jnp.where(allowed, jnp.exp(score - jnp.max(score, axis=1, keepdims=True)), 0.0))
        for expo, qkv in zip(exps, qkvs):
            weights = (expo * (1.0 / jnp.sum(expo, axis=1, keepdims=True))).astype(BF16)
            atts.append(jnp.dot(weights, qkv[:, 2 * span:], preferred_element_type=F32))
        for n in range(heads):
            att = atts[n].astype(BF16).astype(F32)
            hidden = gath[f, :, :, n * span:(n + 1) * span].reshape(total, span).astype(F32)
            fresh = jnp.where(active, hidden + att, hidden).astype(BF16)
            res[:, :, n * span:(n + 1) * span] = fresh.reshape(batches, rows, span)

        links = list(zip(chain[:-1], chain[1:]))
        for a, b in links:
            @pl.when(sec == a)
            def _():
                to_next(b).start()
                cross(1, res.at[0], z, b).start()
        if links:
            @pl.when(sec != chain[-1])
            def _():
                others(lambda chip: relay_line(1, res.at[0], chip).start())
        for s, a in followers.items():
            if a is not None:
                @pl.when(sec == a)
                def _():
                    to_pass(s).start()
        out_ref[...] = res[...]
        for a, b in links:
            @pl.when(sec == a)
            def _():
                relay_cross(1, b)

        others(lambda chip: to_line(chip).wait_send())

        def finish(t, carry):
            to_side(2 * t + core).wait_send()
            return carry

        lax.fori_loop(0, chips, finish, 0)
        for a, b in links:
            @pl.when(sec == a)
            def _():
                to_next(b).wait_send()
                cross(1, res.at[0], z, b).wait_send()
                relay_finish(1, res.at[0], b)
        for s, a in followers.items():
            if a is not None:
                @pl.when(sec == a)
                def _():
                    to_pass(s).wait_send()

    for s, a in followers.items():
        @pl.when(sec == s)
        def _():
            if a is None:
                in_copy().wait()
                out_ref[...] = gath[f]
            else:
                to_pass(s).wait_recv()
                out_ref[...] = res[...]

    @pl.when(sec == helper)
    def _():
        relay_finish(0, in_ref.at[0], chain[0])


def relay(chain, sections, fsdp, collective, inputs, gains, w, count, lengths):
    batches, rows, wide = inputs.shape
    heads, width, cols = w.shape
    pair = 2 if heads % 2 == 0 else 1
    chips = fsdp // 2
    total = batches * rows
    dma = pltpu.SemaphoreType.DMA
    vmem = pl.BlockSpec(memory_space=pltpu.VMEM)
    smem = pl.BlockSpec(memory_space=pltpu.SMEM)
    hbm = pl.BlockSpec(memory_space=pltpu.HBM)
    return pl.pallas_call(
        functools.partial(relay_kernel, chain, sections, fsdp),
        out_shape=jax.ShapeDtypeStruct((batches, rows, wide), BF16),
        in_specs=[hbm, hbm, hbm, smem, smem],
        out_specs=vmem,
        scratch_shapes=[
            pltpu.VMEM(gains.shape, F32),
            pltpu.VMEM((cols // 128, heads, width, 128), BF16),
            pltpu.VMEM((fsdp, batches, rows, wide), BF16),
            pltpu.VMEM((2, chips, rows, wide), BF16),
            pltpu.VMEM((heads // pair, total, pair * cols), F32),
            pltpu.VMEM((total, 1), F32),
            pltpu.VMEM((batches, rows, wide), BF16),
            dma,
            dma((chips, cols // 128)),
            dma,
            dma((batches, fsdp)),
            dma((fsdp,)),
            dma((chips,)),
            dma((chips,)),
            dma((2, chips)),
            dma((2, chips)),
            dma((2, chips)),
            dma,
            dma,
            dma((sections,)),
        ],
        compiler_params=pltpu.CompilerParams(
            collective_id=collective, has_side_effects=True, vmem_limit_bytes=48 * 2**20
        ),
        cost_estimate=pl.CostEstimate(
            flops=2 * total * width * heads * cols, bytes_accessed=2 * heads * width * cols, transcendentals=0
        ),
    )(inputs, gains, w, count, lengths)


def pattern_kernel(sections, count_ref, found_ref, slots, counts, copy_sem, send_sem, recv_sem):
    sec = lax.axis_index("section")
    f = lax.axis_index("fsdp")
    slots[sec] = jnp.full(slots.shape[1:], jnp.where(count_ref[0] > 0, 1, 0), jnp.int32)
    barrier = pltpu.get_barrier_semaphore()
    for k in range(1, sections):
        pl.semaphore_signal(barrier, inc=1, device_id=((sec + k) % sections, f), device_id_type=MESH)
    pl.semaphore_wait(barrier, sections - 1)

    def tell(k):
        return pltpu.make_async_remote_copy(
            src_ref=slots.at[sec], dst_ref=slots.at[sec], send_sem=send_sem.at[k], recv_sem=recv_sem.at[k],
            device_id=((sec + k) % sections, f), device_id_type=MESH)

    for k in range(1, sections):
        tell(k).start()
    for k in range(1, sections):
        tell(k).wait()
    copy = pltpu.make_async_copy(slots, counts, copy_sem)
    copy.start()
    copy.wait()
    found = -1
    for s in range(sections):
        found = found + counts[s, 0, 0] * 2**s
    found_ref[0] = found


def pattern(sections, count):
    dma = pltpu.SemaphoreType.DMA
    found = pl.pallas_call(
        functools.partial(pattern_kernel, sections),
        out_shape=jax.ShapeDtypeStruct((1,), jnp.int32),
        in_specs=[pl.BlockSpec(memory_space=pltpu.SMEM)],
        out_specs=pl.BlockSpec(memory_space=pltpu.SMEM),
        scratch_shapes=[
            pltpu.VMEM((sections, 8, 128), jnp.int32),
            pltpu.SMEM((sections, 8, 128), jnp.int32),
            dma,
            dma((sections,)),
            dma((sections,)),
        ],
        compiler_params=pltpu.CompilerParams(collective_id=0, has_side_effects=True),
    )(count)
    return found[0]


def solution(mesh):
    sections, fsdp = mesh.shape["section"], mesh.shape["fsdp"]

    def per_device(inputs, gains, w_qkv, layer_counts, lengths):
        w = jnp.transpose(w_qkv[0], (1, 0, 2))
        operands = (inputs, gains, w, layer_counts, lengths)
        if sections > 4:
            return relay(tuple(range(sections)), sections, fsdp, 0, *operands)[None]
        branches = []
        for bits in range(1, 2**sections - 1):
            chain = tuple(s for s in range(sections) if bits >> s & 1)
            branches.append(functools.partial(relay, chain, sections, fsdp, bits))
        out = lax.switch(pattern(sections, layer_counts), branches, *operands)
        return out[None]

    in_specs = (
        P(None, None, "fsdp"),
        P("section", None),
        P("section", None, "fsdp", None),
        P("section"),
        P(),
    )
    return jax.shard_map(
        per_device, mesh=mesh, in_specs=in_specs, out_specs=P("section", None, None, "fsdp"), check_vma=False
    )
```

```python
import functools

import jax
import jax.numpy as jnp
from jax import lax
from jax.experimental import pallas as pl
from jax.experimental.pallas import tpu as pltpu
from jax.sharding import PartitionSpec as P

MESH = pl.DeviceIdType.MESH
F32 = jnp.float32
BF16 = jnp.bfloat16


def nearest(t, z, chips):
    near = jnp.minimum(z, chips - 1 - z)
    step = (t + 1) // 2
    both = z + jnp.where(t % 2 == 1, step, -step)
    rest = jnp.where(z <= chips - 1 - z, t, chips - 1 - t)
    return jnp.where(t <= 2 * near, both, rest)


def relay_kernel(
    chain, sections, fsdp,
    in_ref, gain_hbm, w_ref, count_ref, length_ref, out_ref,
    gain_ref, w_vmem, gath, relayed, acc, square, res,
    gain_sem, w_sem, in_sem, recv_sem, side_recv, side_send, line_send,
    relay_recv, relay_send, cross_send, next_send, hop_send, pass_recv, pass_send,
):
    chips = fsdp // 2
    heads, span = w_ref.shape[0], w_ref.shape[2] // 3
    blocks, lanes = w_vmem.shape[0], w_vmem.shape[3]
    total, wide = in_ref.shape
    batches = length_ref.shape[0]
    rows = total // batches
    cuts = (0, total // 4, total * 5 // 8, total)
    parts = [pl.ds(cuts[p], cuts[p + 1] - cuts[p]) for p in range(3)]
    pair = 2 if heads % 2 == 0 else 1
    sec = lax.axis_index("section")
    f = lax.axis_index("fsdp")
    z, core = f // 2, f % 2
    side = 2 * z + 1 - core
    links = list(zip(chain[:-1], chain[1:]))
    bends = [b ^ 2 if b == a ^ 1 else b ^ 1 for a, b in links]
    late = [d in chain and chain.index(d) < k for k, d in enumerate(bends)]
    followers = {}
    for s in range(sections):
        if s not in chain:
            before = [a for a in chain if a < s]
            followers[s] = before[-1] if before else None

    def member(group):
        found = sec == group[0]
        for other in group[1:]:
            found = found | (sec == other)
        return found

    in_chain = member(chain)

    def remote(src, dst, send, recv, target):
        return pltpu.make_async_remote_copy(
            src_ref=src, dst_ref=dst, send_sem=send, recv_sem=recv, device_id=target, device_id_type=MESH)

    def w_copy(chip, c):
        part = pl.ds(pl.multiple_of(chip * 2 * wide, 2 * wide), 2 * wide)
        return pltpu.make_async_copy(
            w_ref.at[:, part, c * lanes:(c + 1) * lanes], w_vmem.at[c, :, part, :], w_sem.at[chip, c])

    def gain_copy():
        return pltpu.make_async_copy(gain_hbm, gain_ref, gain_sem)

    def in_copy():
        return pltpu.make_async_copy(in_ref, gath.at[f], in_sem)

    def to_side(g):
        return remote(gath.at[g], gath.at[g], side_send.at[g // 2], side_recv.at[g], (sec, side))

    def to_line(chip):
        rows_here = gath.at[f, parts[0]]
        return remote(rows_here, rows_here, line_send.at[chip], recv_sem.at[0, f], (sec, 2 * chip + core))

    def arrival(p, g):
        there = gath.at[g, parts[p]]
        return remote(there, there, line_send.at[0], recv_sem.at[p, g], (sec, side))

    def relay_line(turn, src, chip):
        return remote(
            src, relayed.at[turn, z], relay_send.at[turn, chip], relay_recv.at[turn, z], (sec, 2 * chip + core))

    def relay_arrival(turn, chip):
        return remote(
            relayed.at[turn, chip], relayed.at[turn, chip], relay_send.at[turn, chip], relay_recv.at[turn, chip],
            (sec, side))

    def cross(turn, src, chip, b, p):
        g = 2 * chip + core
        return remote(src, gath.at[g, parts[p]], cross_send.at[turn, chip], recv_sem.at[p, g], (b, f))

    def to_next(b):
        return remote(res.at[parts[0]], gath.at[f, parts[0]], next_send, recv_sem.at[0, f], (b, f))

    def to_bend(k):
        return remote(
            res.at[parts[2]], relayed.at[2 + k, z], hop_send, relay_recv.at[2 + k, z], (bends[k], f))

    def to_pass(s):
        return remote(res, res, pass_send.at[s], pass_recv, (s, f))

    def others(body):
        def step(t, carry):
            body(nearest(t, z, chips))
            return carry

        lax.fori_loop(1, chips, step, 0)

    def relay_cross(turn, b, p):
        def body(chip):
            relay_arrival(turn, chip).wait_recv()
            cross(turn, relayed.at[turn, chip], chip, b, p).start()

        others(body)

    def relay_finish(turn, src, b, p):
        def body(chip):
            relay_line(turn, src, chip).wait_send()
            cross(turn, relayed.at[turn, chip], chip, b, p).wait_send()

        others(body)

    def bend(k):
        @pl.when(sec == bends[k])
        def _():
            turn, b = 2 + k, links[k][1]
            mine = relayed.at[turn, z]
            relay_arrival(turn, z).wait_recv()
            cross(turn, mine, z, b, 2).start()
            others(lambda chip: relay_line(turn, mine, chip).start())
            relay_cross(turn, b, 2)

    def bend_finish(k):
        @pl.when(sec == bends[k])
        def _():
            turn, b = 2 + k, links[k][1]
            cross(turn, relayed.at[turn, z], z, b, 2).wait_send()
            relay_finish(turn, relayed.at[turn, z], b, 2)

    fresh_here = member([chain[0]] + [s for s, a in followers.items() if a is None])

    @pl.when(fresh_here)
    def _():
        in_copy().start()

    @pl.when(in_chain)
    def _():
        def begin(t, carry):
            for c in range(blocks):
                w_copy(nearest(t, z, chips), c).start()
            return carry

        gain_copy().start()
        lax.fori_loop(0, chips, begin, 0)

    barrier = pltpu.get_barrier_semaphore()
    pl.semaphore_signal(barrier, inc=1, device_id=(sec, side), device_id_type=MESH)
    others(lambda chip: pl.semaphore_signal(
        barrier, inc=1, device_id=(sec, 2 * chip + core), device_id_type=MESH))
    for k in range(1, sections):
        pl.semaphore_signal(barrier, inc=1, device_id=((sec + k) % sections, f), device_id_type=MESH)
    pl.semaphore_wait(barrier, sections + chips - 1)

    for p in (1, 2):
        @pl.when(sec == chain[0] ^ p)
        def _():
            others(lambda chip: relay_line(0, in_ref.at[parts[p]], chip).start())
            relay_cross(0, chain[0], p)

    for k in range(len(links)):
        if not late[k]:
            bend(k)

    @pl.when(in_chain)
    def _():
        acc[...] = jnp.zeros_like(acc)
        square[...] = jnp.zeros_like(square)
        gain_copy().wait()

        @pl.when(sec == chain[0])
        def _():
            in_copy().wait()

        if len(chain) > 1:
            @pl.when(sec != chain[0])
            def _():
                arrival(0, f).wait_recv()

        others(lambda chip: to_line(chip).start())

        def step(t, carry):
            chip = nearest(t, z, chips)
            g, h = 2 * chip + core, 2 * chip + 1 - core

            @pl.when((t > 0) | (sec != chain[0]))
            def _():
                arrival(1, g).wait_recv()
                arrival(2, g).wait_recv()

            @pl.when(t > 0)
            def _():
                arrival(0, g).wait_recv()

            to_side(g).start()
            for c in range(blocks):
                w_copy(chip, c).wait()
            to_side(h).wait_recv()
            part = pl.ds(pl.multiple_of(chip * 2 * wide, 2 * wide), 2 * wide)
            both = [gath[2 * chip + q].astype(F32) for q in range(2)]
            hidden = jnp.concatenate(both, axis=1)
            square[...] += jnp.sum(hidden * hidden, axis=1, keepdims=True)
            scaled = (hidden * gain_ref[:, part]).astype(BF16)
            for p in range(heads // pair):
                weights = [w_vmem[c, pair * p + q, part, :] for q in range(pair) for c in range(blocks)]
                weights = jnp.concatenate(weights, axis=1)
                acc[p] += jnp.dot(scaled, weights, preferred_element_type=F32)
            return carry

        lax.fori_loop(0, chips, step, 0)

        scale = lax.rsqrt(square[...] / (wide * fsdp) + 1e-05)
        row = lax.broadcasted_iota(jnp.int32, (total, total), 0)
        col = lax.broadcasted_iota(jnp.int32, (total, total), 1)
        allowed = col < 0
        for m in range(batches):
            inside = (row >= m * rows) & (row < (m + 1) * rows) & (col >= m * rows)
            allowed = allowed | (inside & (col < m * rows + length_ref[m]))
        allowed = allowed & (col <= row)
        active = count_ref[0] > 0
        qkvs, exps, atts = [], [], []
        for n in range(heads):
            base = 3 * span * (n % pair)
            qkvs.append((acc[n // pair, :, base:base + 3 * span] * scale).astype(BF16))
        scores = [
            lax.dot_general(
                qkv[:, :span], qkv[:, span:2 * span], (((1,), (1,)), ((), ())), preferred_element_type=F32
            ) for qkv in qkvs
        ]
        for score in scores:
            score = jnp.where(allowed, score * span ** (-0.5), -1e30)
            exps.append(jnp.where(allowed, jnp.exp(score - jnp.max(score, axis=1, keepdims=True)), 0.0))
        for expo, qkv in zip(exps, qkvs):
            weights = (expo * (1.0 / jnp.sum(expo, axis=1, keepdims=True))).astype(BF16)
            atts.append(jnp.dot(weights, qkv[:, 2 * span:], preferred_element_type=F32))
        for n in range(heads):
            att = atts[n].astype(BF16).astype(F32)
            hidden = gath[f, :, n * span:(n + 1) * span].astype(F32)
            fresh = jnp.where(active, hidden + att, hidden).astype(BF16)
            res[:, n * span:(n + 1) * span] = fresh

        for k, (a, b) in enumerate(links):
            @pl.when(sec == a)
            def _():
                to_next(b).start()
                to_bend(k).start()
                cross(1, res.at[parts[1]], z, b, 1).start()
        if links:
            @pl.when(sec != chain[-1])
            def _():
                others(lambda chip: relay_line(1, res.at[parts[1]], chip).start())
        out_ref[...] = res[...]
        for a, b in links:
            @pl.when(sec == a)
            def _():
                relay_cross(1, b, 1)
        for s, a in followers.items():
            if a is not None:
                @pl.when(sec == a)
                def _():
                    to_pass(s).start()

        others(lambda chip: to_line(chip).wait_send())

        def finish(t, carry):
            to_side(2 * t + core).wait_send()
            return carry

        lax.fori_loop(0, chips, finish, 0)
        for k, (a, b) in enumerate(links):
            @pl.when(sec == a)
            def _():
                to_next(b).wait_send()
                to_bend(k).wait_send()
                cross(1, res.at[parts[1]], z, b, 1).wait_send()
                relay_finish(1, res.at[parts[1]], b, 1)
        for s, a in followers.items():
            if a is not None:
                @pl.when(sec == a)
                def _():
                    to_pass(s).wait_send()

    for k in range(len(links)):
        if late[k]:
            bend(k)

    for s, a in followers.items():
        @pl.when(sec == s)
        def _():
            if a is None:
                in_copy().wait()
                out_ref[...] = gath[f]
            else:
                to_pass(s).wait_recv()
                out_ref[...] = res[...]

    for p in (1, 2):
        @pl.when(sec == chain[0] ^ p)
        def _():
            relay_finish(0, in_ref.at[parts[p]], chain[0], p)

    for k in range(len(links)):
        bend_finish(k)


def relay(chain, sections, fsdp, collective, inputs, gains, w, count, lengths):
    batches, rows, wide = inputs.shape
    heads, width, cols = w.shape
    pair = 2 if heads % 2 == 0 else 1
    chips = fsdp // 2
    total = batches * rows
    turns = len(chain) + 1
    dma = pltpu.SemaphoreType.DMA
    vmem = pl.BlockSpec(memory_space=pltpu.VMEM)
    smem = pl.BlockSpec(memory_space=pltpu.SMEM)
    hbm = pl.BlockSpec(memory_space=pltpu.HBM)
    out = pl.pallas_call(
        functools.partial(relay_kernel, chain, sections, fsdp),
        out_shape=jax.ShapeDtypeStruct((total, wide), BF16),
        in_specs=[hbm, hbm, hbm, smem, smem],
        out_specs=vmem,
        scratch_shapes=[
            pltpu.VMEM(gains.shape, F32),
            pltpu.VMEM((cols // 128, heads, width, 128), BF16),
            pltpu.VMEM((fsdp, total, wide), BF16),
            pltpu.VMEM((turns, chips, total * 3 // 8, wide), BF16),
            pltpu.VMEM((heads // pair, total, pair * cols), F32),
            pltpu.VMEM((total, 1), F32),
            pltpu.VMEM((total, wide), BF16),
            dma,
            dma((chips, cols // 128)),
            dma,
            dma((3, fsdp)),
            dma((fsdp,)),
            dma((chips,)),
            dma((chips,)),
            dma((turns, chips)),
            dma((turns, chips)),
            dma((turns, chips)),
            dma,
            dma,
            dma,
            dma((sections,)),
        ],
        compiler_params=pltpu.CompilerParams(
            collective_id=collective, has_side_effects=True, vmem_limit_bytes=48 * 2**20
        ),
        cost_estimate=pl.CostEstimate(
            flops=2 * total * width * heads * cols, bytes_accessed=2 * heads * width * cols, transcendentals=0
        ),
    )(inputs.reshape(total, wide), gains, w, count, lengths)
    return out.reshape(batches, rows, wide)


def pattern_kernel(sections, count_ref, found_ref, slots, counts, copy_sem, send_sem, recv_sem):
    sec = lax.axis_index("section")
    f = lax.axis_index("fsdp")
    slots[sec] = jnp.full(slots.shape[1:], jnp.where(count_ref[0] > 0, 1, 0), jnp.int32)
    barrier = pltpu.get_barrier_semaphore()
    for k in range(1, sections):
        pl.semaphore_signal(barrier, inc=1, device_id=((sec + k) % sections, f), device_id_type=MESH)
    pl.semaphore_wait(barrier, sections - 1)

    def tell(k):
        return pltpu.make_async_remote_copy(
            src_ref=slots.at[sec], dst_ref=slots.at[sec], send_sem=send_sem.at[k], recv_sem=recv_sem.at[k],
            device_id=((sec + k) % sections, f), device_id_type=MESH)

    for k in range(1, sections):
        tell(k).start()
    for k in range(1, sections):
        tell(k).wait()
    copy = pltpu.make_async_copy(slots, counts, copy_sem)
    copy.start()
    copy.wait()
    found = -1
    for s in range(sections):
        found = found + counts[s, 0, 0] * 2**s
    found_ref[0] = found


def pattern(sections, count):
    dma = pltpu.SemaphoreType.DMA
    found = pl.pallas_call(
        functools.partial(pattern_kernel, sections),
        out_shape=jax.ShapeDtypeStruct((1,), jnp.int32),
        in_specs=[pl.BlockSpec(memory_space=pltpu.SMEM)],
        out_specs=pl.BlockSpec(memory_space=pltpu.SMEM),
        scratch_shapes=[
            pltpu.VMEM((sections, 8, 128), jnp.int32),
            pltpu.SMEM((sections, 8, 128), jnp.int32),
            dma,
            dma((sections,)),
            dma((sections,)),
        ],
        compiler_params=pltpu.CompilerParams(collective_id=0, has_side_effects=True),
    )(count)
    return found[0]


def solution(mesh):
    sections, fsdp = mesh.shape["section"], mesh.shape["fsdp"]

    def per_device(inputs, gains, w_qkv, layer_counts, lengths):
        w = jnp.transpose(w_qkv[0], (1, 0, 2))
        operands = (inputs, gains, w, layer_counts, lengths)
        if sections > 4:
            return relay(tuple(range(sections)), sections, fsdp, 0, *operands)[None]
        branches = []
        for bits in range(1, 2**sections - 1):
            chain = tuple(s for s in range(sections) if bits >> s & 1)
            branches.append(functools.partial(relay, chain, sections, fsdp, bits))
        out = lax.switch(pattern(sections, layer_counts), branches, *operands)
        return out[None]

    in_specs = (
        P(None, None, "fsdp"),
        P("section", None),
        P("section", None, "fsdp", None),
        P("section"),
        P(),
    )
    return jax.shard_map(
        per_device, mesh=mesh, in_specs=in_specs, out_specs=P("section", None, None, "fsdp"), check_vma=False
    )
```

```python
import functools

import jax
import jax.numpy as jnp
from jax import lax
from jax.experimental import pallas as pl
from jax.experimental.pallas import tpu as pltpu
from jax.sharding import PartitionSpec as P

MESH = pl.DeviceIdType.MESH
F32 = jnp.float32
BF16 = jnp.bfloat16


def nearest(t, z, chips):
    near = jnp.minimum(z, chips - 1 - z)
    step = (t + 1) // 2
    both = z + jnp.where(t % 2 == 1, step, -step)
    rest = jnp.where(z <= chips - 1 - z, t, chips - 1 - t)
    return jnp.where(t <= 2 * near, both, rest)


def relay_kernel(
    chain, sections, fsdp,
    in_ref, gain_hbm, w_ref, count_ref, length_ref, out_ref,
    gain_ref, w_vmem, gath, relayed, acc, square, res,
    gain_sem, w_sem, in_sem, recv_sem, side_recv, side_send, line_send,
    relay_recv, relay_send, cross_send, next_send, hop_send, pass_recv, pass_send,
):
    chips = fsdp // 2
    heads, span = w_ref.shape[0], w_ref.shape[2] // 3
    blocks, lanes = w_vmem.shape[0], w_vmem.shape[3]
    total, wide = in_ref.shape
    batches = length_ref.shape[0]
    rows = total // batches
    cuts = (0, total // 4, total * 5 // 8, total)
    parts = [pl.ds(cuts[p], cuts[p + 1] - cuts[p]) for p in range(3)]
    pair = 2 if heads % 2 == 0 else 1
    sec = lax.axis_index("section")
    f = lax.axis_index("fsdp")
    z, core = f // 2, f % 2
    side = 2 * z + 1 - core
    links = list(zip(chain[:-1], chain[1:]))
    bends = [b ^ 2 if b == a ^ 1 else b ^ 1 for a, b in links]
    late = [d in chain and chain.index(d) < k for k, d in enumerate(bends)]
    followers = {}
    for s in range(sections):
        if s not in chain:
            before = [a for a in chain if a < s]
            followers[s] = before[-1] if before else None

    def member(group):
        found = sec == group[0]
        for other in group[1:]:
            found = found | (sec == other)
        return found

    in_chain = member(chain)

    def remote(src, dst, send, recv, target):
        return pltpu.make_async_remote_copy(
            src_ref=src, dst_ref=dst, send_sem=send, recv_sem=recv, device_id=target, device_id_type=MESH)

    def w_copy(chip, c):
        part = pl.ds(pl.multiple_of(chip * 2 * wide, 2 * wide), 2 * wide)
        return pltpu.make_async_copy(
            w_ref.at[:, part, c * lanes:(c + 1) * lanes], w_vmem.at[c, :, part, :], w_sem.at[chip, c])

    def gain_copy():
        return pltpu.make_async_copy(gain_hbm, gain_ref, gain_sem)

    def in_copy():
        return pltpu.make_async_copy(in_ref, gath.at[f], in_sem)

    def to_side(g):
        return remote(gath.at[g], gath.at[g], side_send.at[g // 2], side_recv.at[g], (sec, side))

    def to_line(chip):
        rows_here = gath.at[f, parts[0]]
        return remote(rows_here, rows_here, line_send.at[chip], recv_sem.at[0, f], (sec, 2 * chip + core))

    def arrival(p, g):
        there = gath.at[g, parts[p]]
        return remote(there, there, line_send.at[0], recv_sem.at[p, g], (sec, side))

    def relay_line(turn, src, chip):
        return remote(
            src, relayed.at[turn, z], relay_send.at[turn, chip], relay_recv.at[turn, z], (sec, 2 * chip + core))

    def relay_arrival(turn, chip):
        return remote(
            relayed.at[turn, chip], relayed.at[turn, chip], relay_send.at[turn, chip], relay_recv.at[turn, chip],
            (sec, side))

    def cross(turn, src, chip, b, p):
        g = 2 * chip + core
        return remote(src, gath.at[g, parts[p]], cross_send.at[turn, chip], recv_sem.at[p, g], (b, f))

    def to_next(b):
        return remote(res.at[parts[0]], gath.at[f, parts[0]], next_send, recv_sem.at[0, f], (b, f))

    def to_bend(k):
        return remote(
            res.at[parts[2]], relayed.at[2 + k, z], hop_send, relay_recv.at[2 + k, z], (bends[k], f))

    def to_pass(s):
        return remote(res, res, pass_send.at[s], pass_recv, (s, f))

    def others(body):
        def step(t, carry):
            body(nearest(t, z, chips))
            return carry

        lax.fori_loop(1, chips, step, 0)

    def relay_cross(turn, b, p):
        def body(chip):
            relay_arrival(turn, chip).wait_recv()
            cross(turn, relayed.at[turn, chip], chip, b, p).start()

        others(body)

    def relay_finish(turn, src, b, p):
        def body(chip):
            relay_line(turn, src, chip).wait_send()
            cross(turn, relayed.at[turn, chip], chip, b, p).wait_send()

        others(body)

    def bend(k):
        @pl.when(sec == bends[k])
        def _():
            turn, b = 2 + k, links[k][1]
            mine = relayed.at[turn, z]
            relay_arrival(turn, z).wait_recv()
            others(lambda chip: relay_line(turn, mine, chip).start())
            relay_cross(turn, b, 2)

    def bend_finish(k):
        @pl.when(sec == bends[k])
        def _():
            turn, b = 2 + k, links[k][1]
            relay_finish(turn, relayed.at[turn, z], b, 2)

    fresh_here = member([chain[0]] + [s for s, a in followers.items() if a is None])

    @pl.when(fresh_here)
    def _():
        in_copy().start()

    @pl.when(in_chain)
    def _():
        def begin(t, carry):
            for c in range(blocks):
                w_copy(nearest(t, z, chips), c).start()
            return carry

        gain_copy().start()
        lax.fori_loop(0, chips, begin, 0)

    barrier = pltpu.get_barrier_semaphore()
    pl.semaphore_signal(barrier, inc=1, device_id=(sec, side), device_id_type=MESH)
    others(lambda chip: pl.semaphore_signal(
        barrier, inc=1, device_id=(sec, 2 * chip + core), device_id_type=MESH))
    for k in range(1, sections):
        pl.semaphore_signal(barrier, inc=1, device_id=((sec + k) % sections, f), device_id_type=MESH)
    pl.semaphore_wait(barrier, sections + chips - 1)

    for p in (1, 2):
        @pl.when(sec == chain[0] ^ p)
        def _():
            others(lambda chip: relay_line(0, in_ref.at[parts[p]], chip).start())
            relay_cross(0, chain[0], p)

    for k in range(len(links)):
        if not late[k]:
            bend(k)

    @pl.when(in_chain)
    def _():
        acc[...] = jnp.zeros_like(acc)
        square[...] = jnp.zeros_like(square)
        gain_copy().wait()

        @pl.when(sec == chain[0])
        def _():
            in_copy().wait()

        if len(chain) > 1:
            @pl.when(sec != chain[0])
            def _():
                arrival(0, f).wait_recv()

        others(lambda chip: to_line(chip).start())

        def step(t, carry):
            chip = nearest(t, z, chips)
            g, h = 2 * chip + core, 2 * chip + 1 - core

            @pl.when((t > 0) | (sec != chain[0]))
            def _():
                arrival(1, g).wait_recv()
                arrival(2, g).wait_recv()

            @pl.when(t > 0)
            def _():
                arrival(0, g).wait_recv()

            to_side(g).start()
            for c in range(blocks):
                w_copy(chip, c).wait()
            to_side(h).wait_recv()
            part = pl.ds(pl.multiple_of(chip * 2 * wide, 2 * wide), 2 * wide)
            both = [gath[2 * chip + q].astype(F32) for q in range(2)]
            hidden = jnp.concatenate(both, axis=1)
            square[...] += jnp.sum(hidden * hidden, axis=1, keepdims=True)
            scaled = (hidden * gain_ref[:, part]).astype(BF16)
            for p in range(heads // pair):
                weights = [w_vmem[c, pair * p + q, part, :] for q in range(pair) for c in range(blocks)]
                weights = jnp.concatenate(weights, axis=1)
                acc[p] += jnp.dot(scaled, weights, preferred_element_type=F32)
            return carry

        lax.fori_loop(0, chips, step, 0)

        scale = lax.rsqrt(square[...] / (wide * fsdp) + 1e-05)
        row = lax.broadcasted_iota(jnp.int32, (total, total), 0)
        col = lax.broadcasted_iota(jnp.int32, (total, total), 1)
        allowed = col < 0
        for m in range(batches):
            inside = (row >= m * rows) & (row < (m + 1) * rows) & (col >= m * rows)
            allowed = allowed | (inside & (col < m * rows + length_ref[m]))
        allowed = allowed & (col <= row)
        active = count_ref[0] > 0
        qkvs, exps, atts = [], [], []
        for n in range(heads):
            base = 3 * span * (n % pair)
            qkvs.append((acc[n // pair, :, base:base + 3 * span] * scale).astype(BF16))
        scores = [
            lax.dot_general(
                qkv[:, :span], qkv[:, span:2 * span], (((1,), (1,)), ((), ())), preferred_element_type=F32
            ) for qkv in qkvs
        ]
        for score in scores:
            score = jnp.where(allowed, score * span ** (-0.5), -1e30)
            exps.append(jnp.where(allowed, jnp.exp(score - jnp.max(score, axis=1, keepdims=True)), 0.0))
        for expo, qkv in zip(exps, qkvs):
            weights = (expo * (1.0 / jnp.sum(expo, axis=1, keepdims=True))).astype(BF16)
            atts.append(jnp.dot(weights, qkv[:, 2 * span:], preferred_element_type=F32))
        for n in range(heads):
            att = atts[n].astype(BF16).astype(F32)
            hidden = gath[f, :, n * span:(n + 1) * span].astype(F32)
            fresh = jnp.where(active, hidden + att, hidden).astype(BF16)
            res[:, n * span:(n + 1) * span] = fresh

        for k, (a, b) in enumerate(links):
            @pl.when(sec == a)
            def _():
                to_next(b).start()
                cross(1, res.at[parts[1]], z, b, 1).start()
                cross(2 + k, res.at[parts[2]], z, b, 2).start()
                to_bend(k).start()
        if links:
            @pl.when(sec != chain[-1])
            def _():
                others(lambda chip: relay_line(1, res.at[parts[1]], chip).start())
        out_ref[...] = res[...]
        for a, b in links:
            @pl.when(sec == a)
            def _():
                relay_cross(1, b, 1)
        for s, a in followers.items():
            if a is not None:
                @pl.when(sec == a)
                def _():
                    to_pass(s).start()

        others(lambda chip: to_line(chip).wait_send())

        def finish(t, carry):
            to_side(2 * t + core).wait_send()
            return carry

        lax.fori_loop(0, chips, finish, 0)
        for k, (a, b) in enumerate(links):
            @pl.when(sec == a)
            def _():
                to_next(b).wait_send()
                to_bend(k).wait_send()
                cross(1, res.at[parts[1]], z, b, 1).wait_send()
                cross(2 + k, res.at[parts[2]], z, b, 2).wait_send()
                relay_finish(1, res.at[parts[1]], b, 1)
        for s, a in followers.items():
            if a is not None:
                @pl.when(sec == a)
                def _():
                    to_pass(s).wait_send()

    for k in range(len(links)):
        if late[k]:
            bend(k)

    for s, a in followers.items():
        @pl.when(sec == s)
        def _():
            if a is None:
                in_copy().wait()
                out_ref[...] = gath[f]
            else:
                to_pass(s).wait_recv()
                out_ref[...] = res[...]

    for p in (1, 2):
        @pl.when(sec == chain[0] ^ p)
        def _():
            relay_finish(0, in_ref.at[parts[p]], chain[0], p)

    for k in range(len(links)):
        bend_finish(k)


def relay(chain, sections, fsdp, collective, inputs, gains, w, count, lengths):
    batches, rows, wide = inputs.shape
    heads, width, cols = w.shape
    pair = 2 if heads % 2 == 0 else 1
    chips = fsdp // 2
    total = batches * rows
    turns = len(chain) + 1
    dma = pltpu.SemaphoreType.DMA
    vmem = pl.BlockSpec(memory_space=pltpu.VMEM)
    smem = pl.BlockSpec(memory_space=pltpu.SMEM)
    hbm = pl.BlockSpec(memory_space=pltpu.HBM)
    out = pl.pallas_call(
        functools.partial(relay_kernel, chain, sections, fsdp),
        out_shape=jax.ShapeDtypeStruct((total, wide), BF16),
        in_specs=[hbm, hbm, hbm, smem, smem],
        out_specs=vmem,
        scratch_shapes=[
            pltpu.VMEM(gains.shape, F32),
            pltpu.VMEM((cols // 128, heads, width, 128), BF16),
            pltpu.VMEM((fsdp, total, wide), BF16),
            pltpu.VMEM((turns, chips, total * 3 // 8, wide), BF16),
            pltpu.VMEM((heads // pair, total, pair * cols), F32),
            pltpu.VMEM((total, 1), F32),
            pltpu.VMEM((total, wide), BF16),
            dma,
            dma((chips, cols // 128)),
            dma,
            dma((3, fsdp)),
            dma((fsdp,)),
            dma((chips,)),
            dma((chips,)),
            dma((turns, chips)),
            dma((turns, chips)),
            dma((turns, chips)),
            dma,
            dma,
            dma,
            dma((sections,)),
        ],
        compiler_params=pltpu.CompilerParams(
            collective_id=collective, has_side_effects=True, vmem_limit_bytes=48 * 2**20
        ),
        cost_estimate=pl.CostEstimate(
            flops=2 * total * width * heads * cols, bytes_accessed=2 * heads * width * cols, transcendentals=0
        ),
    )(inputs.reshape(total, wide), gains, w, count, lengths)
    return out.reshape(batches, rows, wide)


def pattern_kernel(sections, count_ref, found_ref, slots, counts, copy_sem, send_sem, recv_sem):
    sec = lax.axis_index("section")
    f = lax.axis_index("fsdp")
    slots[sec] = jnp.full(slots.shape[1:], jnp.where(count_ref[0] > 0, 1, 0), jnp.int32)
    barrier = pltpu.get_barrier_semaphore()
    for k in range(1, sections):
        pl.semaphore_signal(barrier, inc=1, device_id=((sec + k) % sections, f), device_id_type=MESH)
    pl.semaphore_wait(barrier, sections - 1)

    def tell(k):
        return pltpu.make_async_remote_copy(
            src_ref=slots.at[sec], dst_ref=slots.at[sec], send_sem=send_sem.at[k], recv_sem=recv_sem.at[k],
            device_id=((sec + k) % sections, f), device_id_type=MESH)

    for k in range(1, sections):
        tell(k).start()
    for k in range(1, sections):
        tell(k).wait()
    copy = pltpu.make_async_copy(slots, counts, copy_sem)
    copy.start()
    copy.wait()
    found = -1
    for s in range(sections):
        found = found + counts[s, 0, 0] * 2**s
    found_ref[0] = found


def pattern(sections, count):
    dma = pltpu.SemaphoreType.DMA
    found = pl.pallas_call(
        functools.partial(pattern_kernel, sections),
        out_shape=jax.ShapeDtypeStruct((1,), jnp.int32),
        in_specs=[pl.BlockSpec(memory_space=pltpu.SMEM)],
        out_specs=pl.BlockSpec(memory_space=pltpu.SMEM),
        scratch_shapes=[
            pltpu.VMEM((sections, 8, 128), jnp.int32),
            pltpu.SMEM((sections, 8, 128), jnp.int32),
            dma,
            dma((sections,)),
            dma((sections,)),
        ],
        compiler_params=pltpu.CompilerParams(collective_id=0, has_side_effects=True),
    )(count)
    return found[0]


def solution(mesh):
    sections, fsdp = mesh.shape["section"], mesh.shape["fsdp"]

    def per_device(inputs, gains, w_qkv, layer_counts, lengths):
        w = jnp.transpose(w_qkv[0], (1, 0, 2))
        operands = (inputs, gains, w, layer_counts, lengths)
        if sections > 4:
            return relay(tuple(range(sections)), sections, fsdp, 0, *operands)[None]
        branches = []
        for bits in range(1, 2**sections - 1):
            chain = tuple(s for s in range(sections) if bits >> s & 1)
            branches.append(functools.partial(relay, chain, sections, fsdp, bits))
        out = lax.switch(pattern(sections, layer_counts), branches, *operands)
        return out[None]

    in_specs = (
        P(None, None, "fsdp"),
        P("section", None),
        P("section", None, "fsdp", None),
        P("section"),
        P(),
    )
    return jax.shard_map(
        per_device, mesh=mesh, in_specs=in_specs, out_specs=P("section", None, None, "fsdp"), check_vma=False
    )
```
